32 devices in a mesh: head: 4 (over x, core), ctx: 2 (over y), inner: 4 (over z).
Axes of the slice: x: 2, y: 2, z: 4, core: 2. Of those that a mesh axis runs over, the one named last changes fastest.
Arguments:
- query_rows: bfloat16 [4096, 48, 128], P(('head', 'ctx', 'inner')), may hold values from -6 to 6
- key_rows: bfloat16 [4096, 48, 128], P(('head', 'ctx', 'inner')), may hold values from -6 to 6
- value_rows: bfloat16 [4096, 48, 128], P(('head', 'ctx', 'inner')), may hold values from -6 to 6
- grad_rows: bfloat16 [4096, 48, 128], P(('head', 'ctx', 'inner')), may hold values from -6 to 6
Outputs:
- grad_query: bfloat16 [4096, 48, 128], P(('head', 'ctx', 'inner'))
- grad_key: bfloat16 [4096, 48, 128], P(('head', 'ctx', 'inner'))
- grad_value: bfloat16 [4096, 48, 128], P(('head', 'ctx', 'inner'))
The draws below stay inside these ranges and needn't reach their ends.
All inputs are finite; a program needn't handle non-finite values.
Results may differ from the reference program's by a relative error of at most 0.012.
The reference program's roundings to bfloat16 on the way count: a program that leaves them out, or rounds other values in their place, can miss the bound.
Values may be sent and summed in bfloat16 or wider, within the bound.
A program may use at most 128 MiB of HBM per device.

```python
import jax
import jax.numpy as jnp
from jax import lax

HEADS = 48
HD = 128
TOK_DEV = 128
SEQ = 4096
SHARDS = 8
BLOCK = 256


def draw_query_rows(key, part):
    base_key = jax.random.fold_in(key, 1)
    drawn = jax.random.truncated_normal(base_key, -6.0, 6.0, (SEQ, HEADS, HD), jnp.float32)
    return drawn.astype(jnp.bfloat16)


def draw_key_rows(key, part):
    base_key = jax.random.fold_in(key, 2)
    drawn = jax.random.truncated_normal(base_key, -6.0, 6.0, (SEQ, HEADS, HD), jnp.float32)
    return drawn.astype(jnp.bfloat16)


def block_levels(rng, shape, pieces, smallest, high):
    level, own = 1.0, jax.random.fold_in(rng, 6)
    for axis_at, blocks in pieces:
        steps = jnp.exp(jax.random.uniform(jax.random.fold_in(own, axis_at), (blocks,), jnp.float32, smallest / len(pieces), high / len(pieces)))
        level = level * jnp.repeat(steps, shape[axis_at] // blocks).reshape([-1 if axis == axis_at else 1 for axis in range(len(shape))])
    return level


def normal_values(own_key, dims, deviation, limit, shards=(), kind=jnp.bfloat16):
    drawn = deviation * jax.random.normal(own_key, dims, jnp.float32)
    if shards:
        drawn = drawn * block_levels(own_key, dims, shards, -0.22, 0.18)
    return jnp.clip(drawn, -limit, limit).astype(kind)


def setup_inputs(seed: int = 0) -> dict:
    keys = jax.random.split(jax.random.key(seed), 5)
    query_rows = draw_query_rows(jax.random.fold_in(keys[4], 71), 0)
    key_rows = draw_key_rows(jax.random.fold_in(keys[4], 71), 0)
    value_rows = normal_values(keys[2], (SEQ, HEADS, HD), 1.0, 6.0, ((0, 32),))
    grad_rows = normal_values(keys[3], (SEQ, HEADS, HD), 1.0, 6.0, ((0, 32),))
    return dict(query_rows=query_rows, key_rows=key_rows, value_rows=value_rows, grad_rows=grad_rows)


def token_positions():
    row_ids = jnp.arange(SEQ, dtype=jnp.int32)
    head_part = row_ids // (TOK_DEV * SHARDS)
    shard_id = (row_ids // TOK_DEV) % SHARDS
    within = head_part * TOK_DEV + row_ids % TOK_DEV
    first_pos = shard_id * BLOCK + within
    second_pos = (2 * SHARDS - 1 - shard_id) * BLOCK + within - BLOCK
    return jnp.where(within < BLOCK, first_pos, second_pos).astype(jnp.int32)


def block_grads(query_block, grad_block, key_prev, value_prev, key_own, value_own, prev_valid):
    score_scale = HD ** -0.5
    query_full = query_block.astype(jnp.float32)
    grad_full = grad_block.astype(jnp.float32)
    key_prev_full = key_prev.astype(jnp.float32)
    value_prev_full = value_prev.astype(jnp.float32)
    key_own_full = key_own.astype(jnp.float32)
    value_own_full = value_own.astype(jnp.float32)
    row_count = query_block.shape[0]
    rows_iota = lax.broadcasted_iota(jnp.int32, (row_count, row_count), 0)
    cols_iota = lax.broadcasted_iota(jnp.int32, (row_count, row_count), 1)
    sees_prev = (cols_iota > rows_iota) & prev_valid
    sees_own = cols_iota <= rows_iota
    scores_prev = jnp.einsum("ihd,jhd->hij", query_full, key_prev_full) * score_scale
    scores_own = jnp.einsum("ihd,jhd->hij", query_full, key_own_full) * score_scale
    row_top = jnp.maximum(jnp.max(jnp.where(sees_prev, scores_prev, -jnp.inf), axis=-1),
                          jnp.max(jnp.where(sees_own, scores_own, -jnp.inf), axis=-1))
    row_total = jnp.sum(jnp.where(sees_prev, jnp.exp(scores_prev - row_top[..., None]), 0.0), axis=-1)
    row_total = row_total + jnp.sum(jnp.where(sees_own, jnp.exp(scores_own - row_top[..., None]), 0.0), axis=-1)
    log_total = row_top + jnp.log(row_total)
    prob_prev = jnp.where(sees_prev, jnp.exp(scores_prev - log_total[..., None]), 0.0)
    prob_own = jnp.where(sees_own, jnp.exp(scores_own - log_total[..., None]), 0.0)
    prob_prev_b = prob_prev.astype(jnp.bfloat16).astype(jnp.float32)
    prob_own_b = prob_own.astype(jnp.bfloat16).astype(jnp.float32)
    attended = jnp.einsum("hij,jhd->ihd", prob_prev_b, value_prev_full) + jnp.einsum("hij,jhd->ihd", prob_own_b, value_own_full)
    row_delta = jnp.sum(grad_full * attended, axis=-1).T
    dprob_prev = jnp.einsum("ihd,jhd->hij", grad_full, value_prev_full)
    dprob_own = jnp.einsum("ihd,jhd->hij", grad_full, value_own_full)
    dscore_prev = (prob_prev * (dprob_prev - row_delta[..., None])).astype(jnp.bfloat16).astype(jnp.float32)
    dscore_own = (prob_own * (dprob_own - row_delta[..., None])).astype(jnp.bfloat16).astype(jnp.float32)
    grad_q = (jnp.einsum("hij,jhd->ihd", dscore_prev, key_prev_full) + jnp.einsum("hij,jhd->ihd", dscore_own, key_own_full)) * score_scale
    grad_k_own = jnp.einsum("hij,ihd->jhd", dscore_own, query_full) * score_scale
    grad_v_own = jnp.einsum("hij,ihd->jhd", prob_own_b, grad_full)
    grad_k_prev = jnp.einsum("hij,ihd->jhd", dscore_prev, query_full) * score_scale
    grad_v_prev = jnp.einsum("hij,ihd->jhd", prob_prev_b, grad_full)
    return grad_q, grad_k_own, grad_v_own, grad_k_prev, grad_v_prev


def reference(query_rows, key_rows, value_rows, grad_rows):
    positions = token_positions()
    seq_order = jnp.zeros((SEQ,), jnp.int32).at[positions].set(jnp.arange(SEQ, dtype=jnp.int32))
    block_total = 2 * SHARDS

    def to_blocks(array):
        return array[seq_order].reshape(block_total, BLOCK, HEADS, HD)

    query_blocks = to_blocks(query_rows)
    key_blocks = to_blocks(key_rows)
    value_blocks = to_blocks(value_rows)
    grad_blocks = to_blocks(grad_rows)
    zero_block = jnp.zeros((1, BLOCK, HEADS, HD), key_rows.dtype)
    key_before = jnp.concatenate([zero_block, key_blocks[:-1]], axis=0)
    value_before = jnp.concatenate([zero_block, value_blocks[:-1]], axis=0)
    prev_flags = jnp.arange(block_total) > 0

    def block_step(carried, inputs):
        query_block, grad_block, key_prev, value_prev, key_own, value_own, prev_valid = inputs
        grad_q, grad_k_own, grad_v_own, grad_k_prev, grad_v_prev = block_grads(
            query_block, grad_block, key_prev, value_prev, key_own, value_own, prev_valid)
        grad_k = grad_k_own + carried[0]
        grad_v = grad_v_own + carried[1]
        return (grad_k_prev, grad_v_prev), (grad_q.astype(jnp.bfloat16), grad_k.astype(jnp.bfloat16), grad_v.astype(jnp.bfloat16))

    start_grads = (jnp.zeros((BLOCK, HEADS, HD), jnp.float32), jnp.zeros((BLOCK, HEADS, HD), jnp.float32))
    inputs = (query_blocks, grad_blocks, key_before, value_before, key_blocks, value_blocks, prev_flags)
    unused, outputs = lax.scan(block_step, start_grads, inputs, reverse=True)
    grad_q_seq = outputs[0].reshape(SEQ, HEADS, HD)
    grad_k_seq = outputs[1].reshape(SEQ, HEADS, HD)
    grad_v_seq = outputs[2].reshape(SEQ, HEADS, HD)
    return grad_q_seq[positions], grad_k_seq[positions], grad_v_seq[positions]
```

```python
import functools

import jax
import jax.numpy as jnp
from jax import lax
from jax.experimental import pallas as pl
from jax.experimental.pallas import tpu as pltpu
from jax.sharding import PartitionSpec as P

MESH = pl.DeviceIdType.MESH
BF16 = jnp.bfloat16
F32 = jnp.float32
CHUNK = 3
LAG = 1
LOW = -1e30


def dot_nt(a, b):
    return lax.dot_general(a, b, (((1,), (1,)), ((), ())), preferred_element_type=F32)


def dot_nn(a, b):
    return lax.dot_general(a, b, (((1,), (0,)), ((), ())), preferred_element_type=F32)


def dot_tn(a, b):
    return lax.dot_general(a, b, (((0,), (0,)), ((), ())), preferred_element_type=F32)


def kernel(
    sizes, x, out, own, prev, acc, partial, arrived, staged,
    kv_send, kv_recv, own_send, own_recv, own_local, grad_send, grad_recv,
    query_send, query_recv, query_local, result_send, result_recv, result_local,
):
    shards, inner = sizes
    heads, rows, width = x.shape[1:]
    mine = heads // 2
    chunks = mine // CHUNK
    scale = width ** -0.5
    log2_scale = scale * 1.4426950408889634

    head_at = lax.axis_index("head")
    shard = lax.axis_index("ctx") * inner + lax.axis_index("inner")
    half = head_at % 2
    other = 1 - half
    block = jnp.where(head_at < 2, shard, 2 * shards - 1 - shard)
    has_prev = block > 0
    has_next = block < 2 * shards - 1

    def device(at, side):
        low = at < shards
        to = jnp.where(low, at, 2 * shards - 1 - at)
        return (jnp.where(low, side, 2 + side), to // inner, to % inner)

    peer = device(block, other)
    after = jnp.where(has_next, block + 1, block - 1)
    before = jnp.where(has_prev, block - 1, block + 1)
    my_rows = pl.ds(pl.multiple_of(half * rows, rows), rows)
    peer_rows = pl.ds(pl.multiple_of(other * rows, rows), rows)

    def kv_copy(c, side):
        return pltpu.make_async_remote_copy(
            x.at[pl.ds(0, 2), pl.ds(side * mine + c * CHUNK, CHUNK)],
            prev.at[:, pl.ds(c * CHUNK, CHUNK), my_rows],
            kv_send.at[side, c], kv_recv.at[half, c], device(after, side), MESH,
        )

    def kv_arrival(c, side):
        return pltpu.make_async_remote_copy(
            x.at[pl.ds(0, 2), pl.ds(c * CHUNK, CHUNK)],
            prev.at[:, pl.ds(c * CHUNK, CHUNK), pl.ds(side * rows, rows)],
            kv_send.at[side, c], kv_recv.at[side, c], device(before, side), MESH,
        )

    def own_copy(c):
        return pltpu.make_async_remote_copy(
            x.at[:, pl.ds(other * mine + c * CHUNK, CHUNK)],
            own.at[:, pl.ds(c * CHUNK, CHUNK), my_rows],
            own_send.at[c], own_recv.at[c], peer, MESH,
        )

    def own_arrival(c):
        return pltpu.make_async_remote_copy(
            x.at[:, pl.ds(other * mine + c * CHUNK, CHUNK)],
            own.at[:, pl.ds(c * CHUNK, CHUNK), peer_rows],
            own_send.at[c], own_recv.at[c], peer, MESH,
        )

    def own_keep(c):
        return pltpu.make_async_copy(
            x.at[:, pl.ds(half * mine + c * CHUNK, CHUNK)],
            own.at[:, pl.ds(c * CHUNK, CHUNK), my_rows],
            own_local.at[c],
        )

    def grad_copy(c, to):
        return pltpu.make_async_remote_copy(
            partial.at[:, pl.ds(c * CHUNK, CHUNK)],
            arrived.at[:, pl.ds(c * CHUNK, CHUNK)],
            grad_send.at[c], grad_recv.at[c], device(to, half), MESH,
        )

    def out_copies(c, first, count, send, recv, local):
        kinds = pl.ds(first, count)
        here = pl.ds(c * CHUNK, CHUNK)
        remote = pltpu.make_async_remote_copy(
            staged.at[kinds, here, peer_rows],
            out.at[kinds, pl.ds(half * mine + c * CHUNK, CHUNK)],
            send.at[c], recv.at[c], peer, MESH,
        )
        arrival = pltpu.make_async_remote_copy(
            staged.at[kinds, here, peer_rows],
            out.at[kinds, pl.ds(other * mine + c * CHUNK, CHUNK)],
            send.at[c], recv.at[c], peer, MESH,
        )
        keep = pltpu.make_async_copy(
            staged.at[kinds, here, my_rows],
            out.at[kinds, pl.ds(half * mine + c * CHUNK, CHUNK)],
            local.at[c],
        )
        return remote, arrival, keep

    def query_out(c):
        return out_copies(c, 0, 1, query_send, query_recv, query_local)

    def result_out(c):
        return out_copies(c, 1, 2, result_send, result_recv, result_local)

    barrier = pltpu.get_barrier_semaphore()
    pl.semaphore_signal(barrier, inc=1, device_id=peer, device_id_type=MESH)

    @pl.when(has_next)
    def _():
        for side in range(2):
            pl.semaphore_signal(barrier, inc=1, device_id=device(after, side), device_id_type=MESH)

    @pl.when(has_prev)
    def _():
        for side in range(2):
            pl.semaphore_signal(barrier, inc=1, device_id=device(before, side), device_id_type=MESH)

    pl.semaphore_wait(
        barrier, 1 + jnp.where(has_next, 2, 0) + jnp.where(has_prev, 2, 0)
    )

    @pl.loop(0, chunks)
    def _(c):
        @pl.when(has_next)
        def _():
            kv_copy(c, 0).start()
            kv_copy(c, 1).start()

        own_copy(c).start()
        own_keep(c).start()

    @pl.when(jnp.logical_not(has_prev))
    def _():
        @pl.loop(0, mine)
        def _(j):
            prev[0, j] = jnp.zeros((2 * rows, width), BF16)
            prev[1, j] = jnp.zeros((2 * rows, width), BF16)

    @pl.when(jnp.logical_not(has_next))
    def _():
        @pl.loop(0, mine)
        def _(j):
            arrived[0, j] = jnp.zeros((2 * rows, width), BF16)
            arrived[1, j] = jnp.zeros((2 * rows, width), BF16)

    row_at = lax.broadcasted_iota(jnp.int32, (2 * rows, 2 * rows), 0)
    column_at = lax.broadcasted_iota(jnp.int32, (2 * rows, 2 * rows), 1)
    sees_own = column_at <= row_at
    sees_prev = column_at > row_at + jnp.where(has_prev, 0, 2 * rows)

    def one_head(j):
        key_prev, value_prev = prev[0, j], prev[1, j]
        key, value, query, grad = own[0, j], own[1, j], own[2, j], own[3, j]
        score_prev = jnp.where(sees_prev, dot_nt(query, key_prev), LOW)
        score_own = jnp.where(sees_own, dot_nt(query, key), LOW)
        top = jnp.maximum(
            jnp.max(score_prev, axis=-1, keepdims=True), jnp.max(score_own, axis=-1, keepdims=True)
        )
        prob_prev = jnp.exp2((score_prev - top) * log2_scale)
        prob_own = jnp.exp2((score_own - top) * log2_scale)
        total = jnp.sum(prob_prev, axis=-1, keepdims=True) + jnp.sum(
            prob_own, axis=-1, keepdims=True
        )
        inverse = 1.0 / total
        prob_prev = prob_prev * inverse
        prob_own = prob_own * inverse
        prob_prev_b = prob_prev.astype(BF16)
        prob_own_b = prob_own.astype(BF16)
        dprob_prev = dot_nt(grad, value_prev)
        dprob_own = dot_nt(grad, value)
        delta = jnp.sum(prob_prev_b.astype(F32) * dprob_prev, axis=-1, keepdims=True) + jnp.sum(
            prob_own_b.astype(F32) * dprob_own, axis=-1, keepdims=True
        )
        dscore_prev = (prob_prev * (dprob_prev - delta)).astype(BF16)
        dscore_own = (prob_own * (dprob_own - delta)).astype(BF16)
        partial[0, j] = (dot_tn(dscore_prev, query) * scale).astype(BF16)
        partial[1, j] = dot_tn(prob_prev_b, grad).astype(BF16)
        staged[0, j] = (
            (dot_nn(dscore_prev, key_prev) + dot_nn(dscore_own, key)) * scale
        ).astype(BF16)
        acc[0, j] = dot_tn(dscore_own, query) * scale
        acc[1, j] = dot_tn(prob_own_b, grad)

    def finish(c):
        @pl.when(has_next)
        def _():
            grad_copy(c, after).wait_recv()

        for at in range(CHUNK):
            j = c * CHUNK + at
            staged[1, j] = (acc[0, j] + arrived[0, j].astype(F32)).astype(BF16)
            staged[2, j] = (acc[1, j] + arrived[1, j].astype(F32)).astype(BF16)
        remote, _, keep = result_out(c)
        remote.start()
        keep.start()

    @pl.loop(0, chunks)
    def _(c):
        own_arrival(c).wait_recv()
        own_keep(c).wait()

        @pl.when(has_prev)
        def _():
            kv_arrival(c, 0).wait_recv()
            kv_arrival(c, 1).wait_recv()

        for at in range(CHUNK):
            one_head(c * CHUNK + at)

        @pl.when(has_prev)
        def _():
            grad_copy(c, before).start()

        remote, _, keep = query_out(c)
        remote.start()
        keep.start()

        @pl.when(c >= LAG)
        def _():
            finish(c - LAG)

    @pl.loop(chunks - LAG, chunks)
    def _(c):
        finish(c)

    @pl.loop(0, chunks)
    def _(c):
        own_copy(c).wait_send()

        @pl.when(has_next)
        def _():
            kv_copy(c, 0).wait_send()
            kv_copy(c, 1).wait_send()

        @pl.when(has_prev)
        def _():
            grad_copy(c, before).wait_send()

        for copies in (query_out(c), result_out(c)):
            remote, arrival, keep = copies
            remote.wait_send()
            arrival.wait_recv()
            keep.wait()


def on_device(shards, inner, query_rows, key_rows, value_rows, grad_rows):
    rows, heads, width = query_rows.shape
    stacked = jnp.stack([key_rows, value_rows, query_rows, grad_rows]).transpose(0, 2, 1, 3)
    mine = heads // 2
    chunks = mine // CHUNK
    dma = pltpu.SemaphoreType.DMA
    result = pl.pallas_call(
        functools.partial(kernel, (shards, inner)),
        out_shape=jax.ShapeDtypeStruct((3, heads, rows, width), BF16),
        in_specs=[pl.BlockSpec(memory_space=pl.ANY)],
        out_specs=pl.BlockSpec(memory_space=pl.ANY),
        scratch_shapes=[
            pltpu.VMEM((4, mine, 2 * rows, width), BF16),
            pltpu.VMEM((2, mine, 2 * rows, width), BF16),
            pltpu.VMEM((2, mine, 2 * rows, width), F32),
            pltpu.VMEM((2, mine, 2 * rows, width), BF16),
            pltpu.VMEM((2, mine, 2 * rows, width), BF16),
            pltpu.VMEM((3, mine, 2 * rows, width), BF16),
            dma((2, chunks)), dma((2, chunks)),
            dma((chunks,)), dma((chunks,)), dma((chunks,)),
            dma((chunks,)), dma((chunks,)),
            dma((chunks,)), dma((chunks,)), dma((chunks,)),
            dma((chunks,)), dma((chunks,)), dma((chunks,)),
        ],
        compiler_params=pltpu.CompilerParams(
            collective_id=0, has_side_effects=True, vmem_limit_bytes=48 * 1024 * 1024
        ),
        cost_estimate=pl.CostEstimate(
            flops=20 * mine * 4 * rows * rows * width,
            bytes_accessed=14 * heads * rows * width,
            transcendentals=mine * 8 * rows * rows,
        ),
    )(stacked)
    result = result.transpose(0, 2, 1, 3)
    return (result[0], result[1], result[2])


def solution(mesh):
    assert mesh.shape["head"] == 4
    shards = mesh.shape["ctx"] * mesh.shape["inner"]
    spec = P(("head", "ctx", "inner"), None, None)
    return jax.shard_map(
        functools.partial(on_device, shards, mesh.shape["inner"]),
        mesh=mesh,
        in_specs=(spec,) * 4,
        out_specs=(spec,) * 3,
        check_vma=False,
    )
```

```python
import functools

import jax
import jax.numpy as jnp
from jax import lax
from jax.experimental import pallas as pl
from jax.experimental.pallas import tpu as pltpu
from jax.sharding import PartitionSpec as P

MESH = pl.DeviceIdType.MESH
BF16 = jnp.bfloat16
F32 = jnp.float32
CHUNK = 2
LAG = 4
LOW = -1e30


def dot_nt(a, b):
    return lax.dot_general(a, b, (((1,), (1,)), ((), ())), preferred_element_type=F32)


def dot_nn(a, b):
    return lax.dot_general(a, b, (((1,), (0,)), ((), ())), preferred_element_type=F32)


def dot_tn(a, b):
    return lax.dot_general(a, b, (((0,), (0,)), ((), ())), preferred_element_type=F32)


def kernel(
    sizes, x, out, own, prev, acc, partial, arrived, staged, relay_kv, relay_grad,
    kv_send, kv_recv, own_send, own_recv, own_local, grad_send, grad_recv,
    query_send, query_recv, query_local, result_send, result_recv, result_local,
    relay_send, relay_recv,
):
    ctx, inner = sizes
    shards = ctx * inner
    heads, rows, width = x.shape[1:]
    mine = heads // 2
    chunks = mine // CHUNK
    scale = width ** -0.5
    log2_scale = scale * 1.4426950408889634

    head_at = lax.axis_index("head")
    ctx_at = lax.axis_index("ctx")
    inner_at = lax.axis_index("inner")
    shard = ctx_at * inner + inner_at
    half = head_at % 2
    other = 1 - half
    block = jnp.where(head_at < 2, shard, 2 * shards - 1 - shard)
    has_prev = block > 0
    has_next = block < 2 * shards - 1

    def device(at, side):
        low = at < shards
        to = jnp.where(low, at, 2 * shards - 1 - at)
        return (jnp.where(low, side, 2 + side), to // inner, to % inner)

    peer = device(block, other)
    after = jnp.where(has_next, block + 1, block - 1)
    before = jnp.where(has_prev, block - 1, block + 1)
    relays = ctx > 1 and inner > 2
    is_first = inner_at == 0
    is_last = inner_at == inner - 1
    low_head = head_at < 2
    can_rise = ctx_at < ctx - 1
    can_fall = ctx_at > 0
    low_corner = jnp.logical_and(is_first, can_rise)
    high_corner = jnp.logical_and(is_last, can_fall)
    wraps_next = jnp.logical_and(has_next, jnp.where(low_head, jnp.logical_and(is_last, can_rise), jnp.logical_and(is_first, can_fall)))
    wraps_prev = jnp.logical_and(has_prev, jnp.where(low_head, jnp.logical_and(is_first, can_fall), jnp.logical_and(is_last, can_rise)))
    kv_relay = jnp.where(low_head, high_corner, low_corner)
    grad_relay = jnp.where(low_head, low_corner, high_corner)
    mirror = inner - 1 - inner_at
    my_rows = pl.ds(pl.multiple_of(half * rows, rows), rows)
    peer_rows = pl.ds(pl.multiple_of(other * rows, rows), rows)

    def kv_copy(c, side):
        return pltpu.make_async_remote_copy(
            x.at[pl.ds(0, 2), pl.ds(side * mine + c * CHUNK, CHUNK)],
            prev.at[:, pl.ds(c * CHUNK, CHUNK), my_rows],
            kv_send.at[side, c], kv_recv.at[half, c], device(after, side), MESH,
        )

    def relay_at(c):
        return pl.ds((c // 2) * CHUNK, CHUNK)

    def kv_detour(c, side):
        return pltpu.make_async_remote_copy(
            x.at[pl.ds(0, 2), pl.ds(side * mine + c * CHUNK, CHUNK)],
            relay_kv.at[side, :, relay_at(c)],
            kv_send.at[side, c], relay_recv.at[side, c // 2],
            (head_at, jnp.where(low_head, ctx_at + 1, ctx_at - 1), inner_at), MESH,
        )

    def kv_forward(c, side):
        return pltpu.make_async_remote_copy(
            relay_kv.at[side, :, relay_at(c)],
            prev.at[:, pl.ds(c * CHUNK, CHUNK), my_rows],
            relay_send.at[side, c // 2], kv_recv.at[half, c],
            (head_at - half + side, ctx_at, mirror), MESH,
        )

    def grad_detour(c):
        return pltpu.make_async_remote_copy(
            partial.at[:, pl.ds(c * CHUNK, CHUNK)],
            relay_grad.at[:, relay_at(c)],
            grad_send.at[c], relay_recv.at[2, c // 2],
            (head_at, jnp.where(low_head, ctx_at - 1, ctx_at + 1), inner_at), MESH,
        )

    def grad_forward(c):
        return pltpu.make_async_remote_copy(
            relay_grad.at[:, relay_at(c)],
            arrived.at[:, pl.ds(c * CHUNK, CHUNK)],
            relay_send.at[2, c // 2], grad_recv.at[c],
            (head_at, ctx_at, mirror), MESH,
        )

    def kv_arrival(c, side):
        return pltpu.make_async_remote_copy(
            x.at[pl.ds(0, 2), pl.ds(c * CHUNK, CHUNK)],
            prev.at[:, pl.ds(c * CHUNK, CHUNK), pl.ds(side * rows, rows)],
            kv_send.at[side, c], kv_recv.at[side, c], device(before, side), MESH,
        )

    def own_copy(c):
        return pltpu.make_async_remote_copy(
            x.at[:, pl.ds(other * mine + c * CHUNK, CHUNK)],
            own.at[:, pl.ds(c * CHUNK, CHUNK), my_rows],
            own_send.at[c], own_recv.at[c], peer, MESH,
        )

    def own_arrival(c):
        return pltpu.make_async_remote_copy(
            x.at[:, pl.ds(other * mine + c * CHUNK, CHUNK)],
            own.at[:, pl.ds(c * CHUNK, CHUNK), peer_rows],
            own_send.at[c], own_recv.at[c], peer, MESH,
        )

    def own_keep(c):
        return pltpu.make_async_copy(
            x.at[:, pl.ds(half * mine + c * CHUNK, CHUNK)],
            own.at[:, pl.ds(c * CHUNK, CHUNK), my_rows],
            own_local.at[c],
        )

    def grad_copy(c, to):
        return pltpu.make_async_remote_copy(
            partial.at[:, pl.ds(c * CHUNK, CHUNK)],
            arrived.at[:, pl.ds(c * CHUNK, CHUNK)],
            grad_send.at[c], grad_recv.at[c], device(to, half), MESH,
        )

    def out_copies(c, first, count, send, recv, local):
        kinds = pl.ds(first, count)
        here = pl.ds(c * CHUNK, CHUNK)
        remote = pltpu.make_async_remote_copy(
            staged.at[kinds, here, peer_rows],
            out.at[kinds, pl.ds(half * mine + c * CHUNK, CHUNK)],
            send.at[c], recv.at[c], peer, MESH,
        )
        arrival = pltpu.make_async_remote_copy(
            staged.at[kinds, here, peer_rows],
            out.at[kinds, pl.ds(other * mine + c * CHUNK, CHUNK)],
            send.at[c], recv.at[c], peer, MESH,
        )
        keep = pltpu.make_async_copy(
            staged.at[kinds, here, my_rows],
            out.at[kinds, pl.ds(half * mine + c * CHUNK, CHUNK)],
            local.at[c],
        )
        return remote, arrival, keep

    def query_out(c):
        return out_copies(c, 0, 1, query_send, query_recv, query_local)

    def result_out(c):
        return out_copies(c, 1, 2, result_send, result_recv, result_local)

    barrier = pltpu.get_barrier_semaphore()
    pl.semaphore_signal(barrier, inc=1, device_id=peer, device_id_type=MESH)

    @pl.when(has_next)
    def _():
        for side in range(2):
            pl.semaphore_signal(barrier, inc=1, device_id=device(after, side), device_id_type=MESH)

    @pl.when(has_prev)
    def _():
        for side in range(2):
            pl.semaphore_signal(barrier, inc=1, device_id=device(before, side), device_id_type=MESH)

    greeted = 1 + jnp.where(has_next, 2, 0) + jnp.where(has_prev, 2, 0)
    if relays:
        corner = jnp.logical_or(is_first, is_last)
        rises = jnp.logical_and(corner, can_rise)
        falls = jnp.logical_and(corner, can_fall)

        @pl.when(corner)
        def _():
            for side in range(2):
                pl.semaphore_signal(
                    barrier, inc=1, device_id=(head_at - half + side, ctx_at, mirror),
                    device_id_type=MESH,
                )

        @pl.when(rises)
        def _():
            pl.semaphore_signal(
                barrier, inc=1, device_id=(head_at, ctx_at + 1, inner_at), device_id_type=MESH
            )

        @pl.when(falls)
        def _():
            pl.semaphore_signal(
                barrier, inc=1, device_id=(head_at, ctx_at - 1, inner_at), device_id_type=MESH
            )

        greeted = greeted + jnp.where(corner, 2, 0)
        greeted = greeted + jnp.where(rises, 1, 0) + jnp.where(falls, 1, 0)
    pl.semaphore_wait(barrier, greeted)

    @pl.loop(0, chunks)
    def _(c):
        detour = jnp.logical_and(wraps_next, c % 2 == 1) if relays else False

        @pl.when(jnp.logical_and(has_next, jnp.logical_not(detour)))
        def _():
            kv_copy(c, 0).start()
            kv_copy(c, 1).start()

        if relays:
            @pl.when(detour)
            def _():
                kv_detour(c, 0).start()
                kv_detour(c, 1).start()

        own_copy(c).start()
        own_keep(c).start()

    @pl.when(jnp.logical_not(has_prev))
    def _():
        @pl.loop(0, mine)
        def _(j):
            prev[0, j] = jnp.zeros((2 * rows, width), BF16)
            prev[1, j] = jnp.zeros((2 * rows, width), BF16)

    @pl.when(jnp.logical_not(has_next))
    def _():
        @pl.loop(0, mine)
        def _(j):
            arrived[0, j] = jnp.zeros((2 * rows, width), BF16)
            arrived[1, j] = jnp.zeros((2 * rows, width), BF16)

    row_at = lax.broadcasted_iota(jnp.int32, (2 * rows, 2 * rows), 0)
    column_at = lax.broadcasted_iota(jnp.int32, (2 * rows, 2 * rows), 1)
    sees_own = column_at <= row_at
    sees_prev = column_at > row_at + jnp.where(has_prev, 0, 2 * rows)

    def one_head(j):
        key_prev, value_prev = prev[0, j], prev[1, j]
        key, value, query, grad = own[0, j], own[1, j], own[2, j], own[3, j]
        score_prev = jnp.where(sees_prev, dot_nt(query, key_prev), LOW)
        score_own = jnp.where(sees_own, dot_nt(query, key), LOW)
        top = jnp.maximum(
            jnp.max(score_prev, axis=-1, keepdims=True), jnp.max(score_own, axis=-1, keepdims=True)
        )
        prob_prev = jnp.exp2((score_prev - top) * log2_scale)
        prob_own = jnp.exp2((score_own - top) * log2_scale)
        total = jnp.sum(prob_prev, axis=-1, keepdims=True) + jnp.sum(
            prob_own, axis=-1, keepdims=True
        )
        inverse = 1.0 / total
        prob_prev = prob_prev * inverse
        prob_own = prob_own * inverse
        prob_prev_b = prob_prev.astype(BF16)
        prob_own_b = prob_own.astype(BF16)
        dprob_prev = dot_nt(grad, value_prev)
        dprob_own = dot_nt(grad, value)
        delta = jnp.sum(prob_prev_b.astype(F32) * dprob_prev, axis=-1, keepdims=True) + jnp.sum(
            prob_own_b.astype(F32) * dprob_own, axis=-1, keepdims=True
        )
        dscore_prev = (prob_prev * (dprob_prev - delta)).astype(BF16)
        dscore_own = (prob_own * (dprob_own - delta)).astype(BF16)
        partial[0, j] = (dot_tn(dscore_prev, query) * scale).astype(BF16)
        partial[1, j] = dot_tn(prob_prev_b, grad).astype(BF16)
        staged[0, j] = (
            (dot_nn(dscore_prev, key_prev) + dot_nn(dscore_own, key)) * scale
        ).astype(BF16)
        acc[0, j] = dot_tn(dscore_own, query) * scale
        acc[1, j] = dot_tn(prob_own_b, grad)

    def finish(c):
        @pl.when(has_next)
        def _():
            grad_copy(c, after).wait_recv()

        for at in range(CHUNK):
            j = c * CHUNK + at
            staged[1, j] = (acc[0, j] + arrived[0, j].astype(F32)).astype(BF16)
            staged[2, j] = (acc[1, j] + arrived[1, j].astype(F32)).astype(BF16)
        remote, _, keep = result_out(c)
        remote.start()
        keep.start()
        if relays:
            @pl.when(jnp.logical_and(grad_relay, c % 2 == 1))
            def _():
                grad_detour(c).wait_recv()
                grad_forward(c).start()

    @pl.loop(0, chunks)
    def _(c):
        own_arrival(c).wait_recv()
        own_keep(c).wait()

        @pl.when(has_prev)
        def _():
            kv_arrival(c, 0).wait_recv()
            kv_arrival(c, 1).wait_recv()

        for at in range(CHUNK):
            one_head(c * CHUNK + at)

        detour = jnp.logical_and(wraps_prev, c % 2 == 1) if relays else False

        @pl.when(jnp.logical_and(has_prev, jnp.logical_not(detour)))
        def _():
            grad_copy(c, before).start()

        if relays:
            @pl.when(detour)
            def _():
                grad_detour(c).start()

            @pl.when(jnp.logical_and(kv_relay, c % 2 == 0))
            def _():
                for side in range(2):
                    kv_detour(c + 1, side).wait_recv()
                    kv_forward(c + 1, side).start()

        remote, _, keep = query_out(c)
        remote.start()
        keep.start()

        @pl.when(c >= LAG)
        def _():
            finish(c - LAG)

    @pl.loop(chunks - LAG, chunks)
    def _(c):
        finish(c)

    @pl.loop(0, chunks)
    def _(c):
        own_copy(c).wait_send()

        @pl.when(has_next)
        def _():
            kv_copy(c, 0).wait_send()
            kv_copy(c, 1).wait_send()

        @pl.when(has_prev)
        def _():
            grad_copy(c, before).wait_send()

        if relays:
            @pl.when(jnp.logical_and(kv_relay, c % 2 == 1))
            def _():
                kv_forward(c, 0).wait_send()
                kv_forward(c, 1).wait_send()

            @pl.when(jnp.logical_and(grad_relay, c % 2 == 1))
            def _():
                grad_forward(c).wait_send()

        for copies in (query_out(c), result_out(c)):
            remote, arrival, keep = copies
            remote.wait_send()
            arrival.wait_recv()
            keep.wait()


def on_device(ctx, inner, query_rows, key_rows, value_rows, grad_rows):
    rows, heads, width = query_rows.shape
    stacked = jnp.stack([key_rows, value_rows, query_rows, grad_rows]).transpose(0, 2, 1, 3)
    mine = heads // 2
    chunks = mine // CHUNK
    dma = pltpu.SemaphoreType.DMA
    result = pl.pallas_call(
        functools.partial(kernel, (ctx, inner)),
        out_shape=jax.ShapeDtypeStruct((3, heads, rows, width), BF16),
        in_specs=[pl.BlockSpec(memory_space=pl.ANY)],
        out_specs=pl.BlockSpec(memory_space=pl.ANY),
        scratch_shapes=[
            pltpu.VMEM((4, mine, 2 * rows, width), BF16),
            pltpu.VMEM((2, mine, 2 * rows, width), BF16),
            pltpu.VMEM((2, mine, 2 * rows, width), F32),
            pltpu.VMEM((2, mine, 2 * rows, width), BF16),
            pltpu.VMEM((2, mine, 2 * rows, width), BF16),
            pltpu.VMEM((3, mine, 2 * rows, width), BF16),
            pltpu.VMEM((2, 2, mine // 2, rows, width), BF16),
            pltpu.VMEM((2, mine // 2, 2 * rows, width), BF16),
            dma((2, chunks)), dma((2, chunks)),
            dma((chunks,)), dma((chunks,)), dma((chunks,)),
            dma((chunks,)), dma((chunks,)),
            dma((chunks,)), dma((chunks,)), dma((chunks,)),
            dma((chunks,)), dma((chunks,)), dma((chunks,)),
            dma((3, chunks // 2)), dma((3, chunks // 2)),
        ],
        compiler_params=pltpu.CompilerParams(
            collective_id=0, has_side_effects=True, vmem_limit_bytes=48 * 1024 * 1024
        ),
        cost_estimate=pl.CostEstimate(
            flops=20 * mine * 4 * rows * rows * width,
            bytes_accessed=14 * heads * rows * width,
            transcendentals=mine * 8 * rows * rows,
        ),
    )(stacked)
    result = result.transpose(0, 2, 1, 3)
    return (result[0], result[1], result[2])


def solution(mesh):
    assert mesh.shape["head"] == 4
    spec = P(("head", "ctx", "inner"), None, None)
    return jax.shard_map(
        functools.partial(on_device, mesh.shape["ctx"], mesh.shape["inner"]),
        mesh=mesh,
        in_specs=(spec,) * 4,
        out_specs=(spec,) * 3,
        check_vma=False,
    )
```

```python
import functools

import jax
import jax.numpy as jnp
from jax import lax
from jax.experimental import pallas as pl
from jax.experimental.pallas import tpu as pltpu
from jax.sharding import PartitionSpec as P

MESH = pl.DeviceIdType.MESH
BF16 = jnp.bfloat16
F32 = jnp.float32
CHUNK = 2
GRAD_LAG = 4
TILE = 16
LOW = -1e30


def dot_nt(a, b):
    return lax.dot_general(a, b, (((1,), (1,)), ((), ())), preferred_element_type=F32)


def dot_nn(a, b):
    return lax.dot_general(a, b, (((1,), (0,)), ((), ())), preferred_element_type=F32)


def dot_tn(a, b):
    return lax.dot_general(a, b, (((0,), (0,)), ((), ())), preferred_element_type=F32)


def kernel(
    sizes, key_rows, value_rows, query_rows, grad_rows, out, raw, x, own, prev, acc, partial, arrived, staged, relay_kv, relay_grad,
    kv_send, kv_recv, own_send, own_recv, own_local, grad_send, grad_recv,
    query_send, query_recv, query_local, result_send, result_recv, result_local,
    relay_send, relay_recv, raw_sem,
):
    ctx, inner = sizes
    shards = ctx * inner
    heads, rows, width = x.shape[1:]
    mine = heads // 2
    chunks = mine // CHUNK
    group = TILE // 2 // CHUNK
    scale = width ** -0.5
    log2_scale = scale * 1.4426950408889634

    head_at = lax.axis_index("head")
    ctx_at = lax.axis_index("ctx")
    inner_at = lax.axis_index("inner")
    shard = ctx_at * inner + inner_at
    half = head_at % 2
    other = 1 - half
    block = jnp.where(head_at < 2, shard, 2 * shards - 1 - shard)
    has_prev = block > 0
    has_next = block < 2 * shards - 1

    inputs = (key_rows, value_rows, query_rows, grad_rows)

    def load(kind):
        return pltpu.make_async_copy(inputs[kind], raw.at[kind], raw_sem.at[kind])

    def heads_of(side, c):
        return pl.ds((c // group) * TILE + side * (TILE // 2) + (c % group) * CHUNK, CHUNK)

    def device(at, side):
        low = at < shards
        to = jnp.where(low, at, 2 * shards - 1 - at)
        return (jnp.where(low, side, 2 + side), to // inner, to % inner)

    peer = device(block, other)
    after = jnp.where(has_next, block + 1, block - 1)
    before = jnp.where(has_prev, block - 1, block + 1)
    relays = ctx > 1 and inner > 2
    is_first = inner_at == 0
    is_last = inner_at == inner - 1
    low_head = head_at < 2
    can_rise = ctx_at < ctx - 1
    can_fall = ctx_at > 0
    low_corner = jnp.logical_and(is_first, can_rise)
    high_corner = jnp.logical_and(is_last, can_fall)
    wraps_next = jnp.logical_and(has_next, jnp.where(low_head, jnp.logical_and(is_last, can_rise), jnp.logical_and(is_first, can_fall)))
    wraps_prev = jnp.logical_and(has_prev, jnp.where(low_head, jnp.logical_and(is_first, can_fall), jnp.logical_and(is_last, can_rise)))
    kv_relay = jnp.where(low_head, high_corner, low_corner)
    grad_relay = jnp.where(low_head, low_corner, high_corner)
    mirror = inner - 1 - inner_at
    my_rows = pl.ds(pl.multiple_of(half * rows, rows), rows)
    peer_rows = pl.ds(pl.multiple_of(other * rows, rows), rows)

    def kv_copy(c, side):
        return pltpu.make_async_remote_copy(
            x.at[pl.ds(0, 2), heads_of(side, c)],
            prev.at[:, pl.ds(c * CHUNK, CHUNK), my_rows],
            kv_send.at[side, c], kv_recv.at[half, c], device(after, side), MESH,
        )

    def relay_at(c):
        return pl.ds((c // 2) * CHUNK, CHUNK)

    def kv_detour(c, side):
        return pltpu.make_async_remote_copy(
            x.at[pl.ds(0, 2), heads_of(side, c)],
            relay_kv.at[side, :, relay_at(c)],
            kv_send.at[side, c], relay_recv.at[side, c // 2],
            (head_at, jnp.where(low_head, ctx_at + 1, ctx_at - 1), inner_at), MESH,
        )

    def kv_forward(c, side):
        return pltpu.make_async_remote_copy(
            relay_kv.at[side, :, relay_at(c)],
            prev.at[:, pl.ds(c * CHUNK, CHUNK), my_rows],
            relay_send.at[side, c // 2], kv_recv.at[half, c],
            (head_at - half + side, ctx_at, mirror), MESH,
        )

    def grad_detour(c):
        return pltpu.make_async_remote_copy(
            partial.at[:, pl.ds(c * CHUNK, CHUNK)],
            relay_grad.at[:, relay_at(c)],
            grad_send.at[c], relay_recv.at[2, c // 2],
            (head_at, jnp.where(low_head, ctx_at - 1, ctx_at + 1), inner_at), MESH,
        )

    def grad_forward(c):
        return pltpu.make_async_remote_copy(
            relay_grad.at[:, relay_at(c)],
            arrived.at[:, pl.ds(c * CHUNK, CHUNK)],
            relay_send.at[2, c // 2], grad_recv.at[c],
            (head_at, ctx_at, mirror), MESH,
        )

    def kv_arrival(c, side):
        return pltpu.make_async_remote_copy(
            x.at[pl.ds(0, 2), heads_of(side, c)],
            prev.at[:, pl.ds(c * CHUNK, CHUNK), pl.ds(side * rows, rows)],
            kv_send.at[side, c], kv_recv.at[side, c], device(before, side), MESH,
        )

    def own_copy(c):
        return pltpu.make_async_remote_copy(
            x.at[:, heads_of(other, c)],
            own.at[:, pl.ds(c * CHUNK, CHUNK), my_rows],
            own_send.at[c], own_recv.at[c], peer, MESH,
        )

    def own_arrival(c):
        return pltpu.make_async_remote_copy(
            x.at[:, heads_of(other, c)],
            own.at[:, pl.ds(c * CHUNK, CHUNK), peer_rows],
            own_send.at[c], own_recv.at[c], peer, MESH,
        )

    def own_keep(c):
        return pltpu.make_async_copy(
            x.at[:, heads_of(half, c)],
            own.at[:, pl.ds(c * CHUNK, CHUNK), my_rows],
            own_local.at[c],
        )

    def grad_copy(c, to):
        return pltpu.make_async_remote_copy(
            partial.at[:, pl.ds(c * CHUNK, CHUNK)],
            arrived.at[:, pl.ds(c * CHUNK, CHUNK)],
            grad_send.at[c], grad_recv.at[c], device(to, half), MESH,
        )

    def out_copies(c, first, count, send, recv, local):
        kinds = pl.ds(first, count)
        here = pl.ds(c * CHUNK, CHUNK)
        remote = pltpu.make_async_remote_copy(
            staged.at[kinds, here, peer_rows],
            out.at[kinds, heads_of(half, c)],
            send.at[c], recv.at[c], peer, MESH,
        )
        arrival = pltpu.make_async_remote_copy(
            staged.at[kinds, here, peer_rows],
            out.at[kinds, heads_of(other, c)],
            send.at[c], recv.at[c], peer, MESH,
        )
        keep = pltpu.make_async_copy(
            staged.at[kinds, here, my_rows],
            out.at[kinds, heads_of(half, c)],
            local.at[c],
        )
        return remote, arrival, keep

    def query_out(c):
        return out_copies(c, 0, 1, query_send, query_recv, query_local)

    def result_out(c):
        return out_copies(c, 1, 2, result_send, result_recv, result_local)

    for kind in range(4):
        load(kind).start()

    barrier = pltpu.get_barrier_semaphore()
    pl.semaphore_signal(barrier, inc=1, device_id=peer, device_id_type=MESH)

    @pl.when(has_next)
    def _():
        for side in range(2):
            pl.semaphore_signal(barrier, inc=1, device_id=device(after, side), device_id_type=MESH)

    @pl.when(has_prev)
    def _():
        for side in range(2):
            pl.semaphore_signal(barrier, inc=1, device_id=device(before, side), device_id_type=MESH)

    greeted = 1 + jnp.where(has_next, 2, 0) + jnp.where(has_prev, 2, 0)
    if relays:
        corner = jnp.logical_or(is_first, is_last)
        rises = jnp.logical_and(corner, can_rise)
        falls = jnp.logical_and(corner, can_fall)

        @pl.when(corner)
        def _():
            for side in range(2):
                pl.semaphore_signal(
                    barrier, inc=1, device_id=(head_at - half + side, ctx_at, mirror),
                    device_id_type=MESH,
                )

        @pl.when(rises)
        def _():
            pl.semaphore_signal(
                barrier, inc=1, device_id=(head_at, ctx_at + 1, inner_at), device_id_type=MESH
            )

        @pl.when(falls)
        def _():
            pl.semaphore_signal(
                barrier, inc=1, device_id=(head_at, ctx_at - 1, inner_at), device_id_type=MESH
            )

        greeted = greeted + jnp.where(corner, 2, 0)
        greeted = greeted + jnp.where(rises, 1, 0) + jnp.where(falls, 1, 0)
    pl.semaphore_wait(barrier, greeted)

    def send_kv(c):
        detour = jnp.logical_and(wraps_next, c % 2 == 1) if relays else False

        @pl.when(jnp.logical_and(has_next, jnp.logical_not(detour)))
        def _():
            kv_copy(c, 0).start()
            kv_copy(c, 1).start()

        if relays:
            @pl.when(detour)
            def _():
                kv_detour(c, 0).start()
                kv_detour(c, 1).start()

    def turn(kind, g):
        here = pl.ds(pl.multiple_of(g * TILE, TILE), TILE)
        x[kind, here] = jnp.swapaxes(raw[kind, :, here, :], 0, 1)

    for kind in range(4):
        load(kind).wait()

    @pl.loop(0, heads // TILE)
    def _(g):
        turn(0, g)
        turn(1, g)

        @pl.loop(0, group)
        def _(at):
            send_kv(g * group + at)

        turn(2, g)
        turn(3, g)

        @pl.loop(0, group)
        def _(at):
            own_copy(g * group + at).start()
            own_keep(g * group + at).start()

    @pl.when(jnp.logical_not(has_prev))
    def _():
        @pl.loop(0, mine)
        def _(j):
            prev[0, j] = jnp.zeros((2 * rows, width), BF16)
            prev[1, j] = jnp.zeros((2 * rows, width), BF16)

    @pl.when(jnp.logical_not(has_next))
    def _():
        @pl.loop(0, mine)
        def _(j):
            arrived[0, j] = jnp.zeros((2 * rows, width), BF16)
            arrived[1, j] = jnp.zeros((2 * rows, width), BF16)

    row_at = lax.broadcasted_iota(jnp.int32, (2 * rows, 2 * rows), 0)
    column_at = lax.broadcasted_iota(jnp.int32, (2 * rows, 2 * rows), 1)
    sees_own = column_at <= row_at
    sees_prev = column_at > row_at + jnp.where(has_prev, 0, 2 * rows)

    def one_head(j):
        key_prev, value_prev = prev[0, j], prev[1, j]
        key, value, query, grad = own[0, j], own[1, j], own[2, j], own[3, j]
        score_prev = jnp.where(sees_prev, dot_nt(query, key_prev), LOW)
        score_own = jnp.where(sees_own, dot_nt(query, key), LOW)
        top = jnp.maximum(
            jnp.max(score_prev, axis=-1, keepdims=True), jnp.max(score_own, axis=-1, keepdims=True)
        )
        prob_prev = jnp.exp2((score_prev - top) * log2_scale)
        prob_own = jnp.exp2((score_own - top) * log2_scale)
        total = jnp.sum(prob_prev, axis=-1, keepdims=True) + jnp.sum(
            prob_own, axis=-1, keepdims=True
        )
        inverse = 1.0 / total
        prob_prev = prob_prev * inverse
        prob_own = prob_own * inverse
        prob_prev_b = prob_prev.astype(BF16)
        prob_own_b = prob_own.astype(BF16)
        dprob_prev = dot_nt(grad, value_prev)
        dprob_own = dot_nt(grad, value)
        delta = jnp.sum(prob_prev_b.astype(F32) * dprob_prev, axis=-1, keepdims=True) + jnp.sum(
            prob_own_b.astype(F32) * dprob_own, axis=-1, keepdims=True
        )
        dscore_prev = (prob_prev * (dprob_prev - delta)).astype(BF16)
        dscore_own = (prob_own * (dprob_own - delta)).astype(BF16)
        partial[0, j] = (dot_tn(dscore_prev, query) * scale).astype(BF16)
        partial[1, j] = dot_tn(prob_prev_b, grad).astype(BF16)
        staged[0, j] = (
            (dot_nn(dscore_prev, key_prev) + dot_nn(dscore_own, key)) * scale
        ).astype(BF16)
        acc[0, j] = dot_tn(dscore_own, query) * scale
        acc[1, j] = dot_tn(prob_own_b, grad)

    def finish(c):
        @pl.when(has_next)
        def _():
            grad_copy(c, after).wait_recv()

        for at in range(CHUNK):
            j = c * CHUNK + at
            staged[1, j] = (acc[0, j] + arrived[0, j].astype(F32)).astype(BF16)
            staged[2, j] = (acc[1, j] + arrived[1, j].astype(F32)).astype(BF16)
        remote, _, keep = result_out(c)
        remote.start()
        keep.start()

    def forward_grad(c):
        @pl.when(jnp.logical_and(grad_relay, c % 2 == 0))
        def _():
            grad_detour(c).wait_recv()
            grad_forward(c).start()

    @pl.loop(0, chunks)
    def _(c):
        own_arrival(c).wait_recv()
        own_keep(c).wait()

        @pl.when(has_prev)
        def _():
            kv_arrival(c, 0).wait_recv()
            kv_arrival(c, 1).wait_recv()

        for at in range(CHUNK):
            one_head(c * CHUNK + at)

        detour = jnp.logical_and(wraps_prev, c % 2 == 0) if relays else False

        @pl.when(jnp.logical_and(has_prev, jnp.logical_not(detour)))
        def _():
            grad_copy(c, before).start()

        if relays:
            @pl.when(detour)
            def _():
                grad_detour(c).start()

            @pl.when(jnp.logical_and(kv_relay, c % 2 == 0))
            def _():
                for side in range(2):
                    kv_detour(c + 1, side).wait_recv()
                    kv_forward(c + 1, side).start()

        remote, _, keep = query_out(c)
        remote.start()
        keep.start()

        if relays:
            @pl.when(c >= GRAD_LAG)
            def _():
                forward_grad(c - GRAD_LAG)

    if relays:
        @pl.loop(chunks - GRAD_LAG, chunks)
        def _(c):
            forward_grad(c)

    @pl.loop(0, chunks)
    def _(c):
        finish(c)

    @pl.loop(0, chunks)
    def _(c):
        own_copy(c).wait_send()

        @pl.when(has_next)
        def _():
            kv_copy(c, 0).wait_send()
            kv_copy(c, 1).wait_send()

        @pl.when(has_prev)
        def _():
            grad_copy(c, before).wait_send()

        if relays:
            @pl.when(jnp.logical_and(kv_relay, c % 2 == 1))
            def _():
                kv_forward(c, 0).wait_send()
                kv_forward(c, 1).wait_send()

            @pl.when(jnp.logical_and(grad_relay, c % 2 == 0))
            def _():
                grad_forward(c).wait_send()

        for copies in (query_out(c), result_out(c)):
            remote, arrival, keep = copies
            remote.wait_send()
            arrival.wait_recv()
            keep.wait()


def on_device(ctx, inner, query_rows, key_rows, value_rows, grad_rows):
    rows, heads, width = query_rows.shape
    mine = heads // 2
    chunks = mine // CHUNK
    dma = pltpu.SemaphoreType.DMA
    result = pl.pallas_call(
        functools.partial(kernel, (ctx, inner)),
        out_shape=jax.ShapeDtypeStruct((3, heads, rows, width), BF16),
        in_specs=[pl.BlockSpec(memory_space=pl.ANY)] * 4,
        out_specs=pl.BlockSpec(memory_space=pl.ANY),
        scratch_shapes=[
            pltpu.VMEM((4, rows, heads, width), BF16),
            pltpu.VMEM((4, heads, rows, width), BF16),
            pltpu.VMEM((4, mine, 2 * rows, width), BF16),
            pltpu.VMEM((2, mine, 2 * rows, width), BF16),
            pltpu.VMEM((2, mine, 2 * rows, width), F32),
            pltpu.VMEM((2, mine, 2 * rows, width), BF16),
            pltpu.VMEM((2, mine, 2 * rows, width), BF16),
            pltpu.VMEM((3, mine, 2 * rows, width), BF16),
            pltpu.VMEM((2, 2, mine // 2, rows, width), BF16),
            pltpu.VMEM((2, mine // 2, 2 * rows, width), BF16),
            dma((2, chunks)), dma((2, chunks)),
            dma((chunks,)), dma((chunks,)), dma((chunks,)),
            dma((chunks,)), dma((chunks,)),
            dma((chunks,)), dma((chunks,)), dma((chunks,)),
            dma((chunks,)), dma((chunks,)), dma((chunks,)),
            dma((3, chunks // 2)), dma((3, chunks // 2)), dma((4,)),
        ],
        compiler_params=pltpu.CompilerParams(
            collective_id=0, has_side_effects=True, vmem_limit_bytes=56 * 1024 * 1024
        ),
        cost_estimate=pl.CostEstimate(
            flops=20 * mine * 4 * rows * rows * width,
            bytes_accessed=14 * heads * rows * width,
            transcendentals=mine * 8 * rows * rows,
        ),
    )(key_rows, value_rows, query_rows, grad_rows)
    result = result.transpose(0, 2, 1, 3)
    return (result[0], result[1], result[2])


def solution(mesh):
    assert mesh.shape["head"] == 4
    spec = P(("head", "ctx", "inner"), None, None)
    return jax.shard_map(
        functools.partial(on_device, mesh.shape["ctx"], mesh.shape["inner"]),
        mesh=mesh,
        in_specs=(spec,) * 4,
        out_specs=(spec,) * 3,
        check_vma=False,
    )
```

```python
import functools

import jax
import jax.numpy as jnp
from jax import lax
from jax.experimental import pallas as pl
from jax.experimental.pallas import tpu as pltpu
from jax.sharding import PartitionSpec as P

MESH = pl.DeviceIdType.MESH
BF16 = jnp.bfloat16
F32 = jnp.float32
CHUNK = 2
GRAD_LAG = 4
TILE = 16
LOW = -1e30


def dot_nt(a, b):
    return lax.dot_general(a, b, (((1,), (1,)), ((), ())), preferred_element_type=F32)


def dot_nn(a, b):
    return lax.dot_general(a, b, (((1,), (0,)), ((), ())), preferred_element_type=F32)


def dot_tn(a, b):
    return lax.dot_general(a, b, (((0,), (0,)), ((), ())), preferred_element_type=F32)


def kernel(
    sizes, key_rows, value_rows, query_rows, grad_rows, grad_query, grad_key, grad_value,
    raw, x, out, own, prev, acc, partial, arrived, staged, relay_kv, relay_grad,
    kv_send, kv_recv, own_send, own_recv, own_local, grad_send, grad_recv,
    query_send, query_recv, query_local, result_send, result_recv, result_local,
    relay_send, relay_recv, raw_sem, turned_sem,
):
    ctx, inner = sizes
    shards = ctx * inner
    heads, rows, width = x.shape[1:]
    mine = heads // 2
    chunks = mine // CHUNK
    group = TILE // 2 // CHUNK
    scale = width ** -0.5
    log2_scale = scale * 1.4426950408889634

    head_at = lax.axis_index("head")
    ctx_at = lax.axis_index("ctx")
    inner_at = lax.axis_index("inner")
    shard = ctx_at * inner + inner_at
    half = head_at % 2
    other = 1 - half
    block = jnp.where(head_at < 2, shard, 2 * shards - 1 - shard)
    has_prev = block > 0
    has_next = block < 2 * shards - 1

    inputs = (key_rows, value_rows, query_rows, grad_rows)

    def load(kind):
        return pltpu.make_async_copy(inputs[kind], raw.at[kind], raw_sem.at[kind])

    def heads_of(side, c):
        return pl.ds((c // group) * TILE + side * (TILE // 2) + (c % group) * CHUNK, CHUNK)

    def device(at, side):
        low = at < shards
        to = jnp.where(low, at, 2 * shards - 1 - at)
        return (jnp.where(low, side, 2 + side), to // inner, to % inner)

    peer = device(block, other)
    after = jnp.where(has_next, block + 1, block - 1)
    before = jnp.where(has_prev, block - 1, block + 1)
    relays = ctx > 1 and inner > 2
    is_first = inner_at == 0
    is_last = inner_at == inner - 1
    low_head = head_at < 2
    can_rise = ctx_at < ctx - 1
    can_fall = ctx_at > 0
    low_corner = jnp.logical_and(is_first, can_rise)
    high_corner = jnp.logical_and(is_last, can_fall)
    wraps_next = jnp.logical_and(has_next, jnp.where(low_head, jnp.logical_and(is_last, can_rise), jnp.logical_and(is_first, can_fall)))
    wraps_prev = jnp.logical_and(has_prev, jnp.where(low_head, jnp.logical_and(is_first, can_fall), jnp.logical_and(is_last, can_rise)))
    kv_relay = jnp.where(low_head, high_corner, low_corner)
    grad_relay = jnp.where(low_head, low_corner, high_corner)
    mirror = inner - 1 - inner_at
    my_rows = pl.ds(pl.multiple_of(half * rows, rows), rows)
    peer_rows = pl.ds(pl.multiple_of(other * rows, rows), rows)

    def kv_copy(c, side):
        return pltpu.make_async_remote_copy(
            x.at[pl.ds(0, 2), heads_of(side, c)],
            prev.at[:, pl.ds(c * CHUNK, CHUNK), my_rows],
            kv_send.at[side, c], kv_recv.at[half, c], device(after, side), MESH,
        )

    def relay_at(c):
        return pl.ds((c // 2) * CHUNK, CHUNK)

    def kv_detour(c, side):
        return pltpu.make_async_remote_copy(
            x.at[pl.ds(0, 2), heads_of(side, c)],
            relay_kv.at[side, :, relay_at(c)],
            kv_send.at[side, c], relay_recv.at[side, c // 2],
            (head_at, jnp.where(low_head, ctx_at + 1, ctx_at - 1), inner_at), MESH,
        )

    def kv_forward(c, side):
        return pltpu.make_async_remote_copy(
            relay_kv.at[side, :, relay_at(c)],
            prev.at[:, pl.ds(c * CHUNK, CHUNK), my_rows],
            relay_send.at[side, c // 2], kv_recv.at[half, c],
            (head_at - half + side, ctx_at, mirror), MESH,
        )

    def grad_detour(c):
        return pltpu.make_async_remote_copy(
            partial.at[:, pl.ds(c * CHUNK, CHUNK)],
            relay_grad.at[:, relay_at(c)],
            grad_send.at[c], relay_recv.at[2, c // 2],
            (head_at, jnp.where(low_head, ctx_at - 1, ctx_at + 1), inner_at), MESH,
        )

    def grad_forward(c):
        return pltpu.make_async_remote_copy(
            relay_grad.at[:, relay_at(c)],
            arrived.at[:, pl.ds(c * CHUNK, CHUNK)],
            relay_send.at[2, c // 2], grad_recv.at[c],
            (head_at, ctx_at, mirror), MESH,
        )

    def kv_arrival(c, side):
        return pltpu.make_async_remote_copy(
            x.at[pl.ds(0, 2), heads_of(side, c)],
            prev.at[:, pl.ds(c * CHUNK, CHUNK), pl.ds(side * rows, rows)],
            kv_send.at[side, c], kv_recv.at[side, c], device(before, side), MESH,
        )

    def own_copy(c):
        return pltpu.make_async_remote_copy(
            x.at[:, heads_of(other, c)],
            own.at[:, pl.ds(c * CHUNK, CHUNK), my_rows],
            own_send.at[c], own_recv.at[c], peer, MESH,
        )

    def own_arrival(c):
        return pltpu.make_async_remote_copy(
            x.at[:, heads_of(other, c)],
            own.at[:, pl.ds(c * CHUNK, CHUNK), peer_rows],
            own_send.at[c], own_recv.at[c], peer, MESH,
        )

    def own_keep(c):
        return pltpu.make_async_copy(
            x.at[:, heads_of(half, c)],
            own.at[:, pl.ds(c * CHUNK, CHUNK), my_rows],
            own_local.at[c],
        )

    def grad_copy(c, to):
        return pltpu.make_async_remote_copy(
            partial.at[:, pl.ds(c * CHUNK, CHUNK)],
            arrived.at[:, pl.ds(c * CHUNK, CHUNK)],
            grad_send.at[c], grad_recv.at[c], device(to, half), MESH,
        )

    def out_copies(c, first, count, send, recv, local):
        kinds = pl.ds(first, count)
        here = pl.ds(c * CHUNK, CHUNK)
        remote = pltpu.make_async_remote_copy(
            staged.at[kinds, here, peer_rows],
            out.at[kinds, heads_of(half, c)],
            send.at[c], recv.at[c], peer, MESH,
        )
        arrival = pltpu.make_async_remote_copy(
            staged.at[kinds, here, peer_rows],
            out.at[kinds, heads_of(other, c)],
            send.at[c], recv.at[c], peer, MESH,
        )
        keep = pltpu.make_async_copy(
            staged.at[kinds, here, my_rows],
            out.at[kinds, heads_of(half, c)],
            local.at[c],
        )
        return remote, arrival, keep

    def query_out(c):
        return out_copies(c, 0, 1, query_send, query_recv, query_local)

    def result_out(c):
        return out_copies(c, 1, 2, result_send, result_recv, result_local)

    for kind in range(4):
        load(kind).start()

    barrier = pltpu.get_barrier_semaphore()
    pl.semaphore_signal(barrier, inc=1, device_id=peer, device_id_type=MESH)

    @pl.when(has_next)
    def _():
        for side in range(2):
            pl.semaphore_signal(barrier, inc=1, device_id=device(after, side), device_id_type=MESH)

    @pl.when(has_prev)
    def _():
        for side in range(2):
            pl.semaphore_signal(barrier, inc=1, device_id=device(before, side), device_id_type=MESH)

    greeted = 1 + jnp.where(has_next, 2, 0) + jnp.where(has_prev, 2, 0)
    if relays:
        corner = jnp.logical_or(is_first, is_last)
        rises = jnp.logical_and(corner, can_rise)
        falls = jnp.logical_and(corner, can_fall)

        @pl.when(corner)
        def _():
            for side in range(2):
                pl.semaphore_signal(
                    barrier, inc=1, device_id=(head_at - half + side, ctx_at, mirror),
                    device_id_type=MESH,
                )

        @pl.when(rises)
        def _():
            pl.semaphore_signal(
                barrier, inc=1, device_id=(head_at, ctx_at + 1, inner_at), device_id_type=MESH
            )

        @pl.when(falls)
        def _():
            pl.semaphore_signal(
                barrier, inc=1, device_id=(head_at, ctx_at - 1, inner_at), device_id_type=MESH
            )

        greeted = greeted + jnp.where(corner, 2, 0)
        greeted = greeted + jnp.where(rises, 1, 0) + jnp.where(falls, 1, 0)
    pl.semaphore_wait(barrier, greeted)

    def send_kv(c):
        detour = jnp.logical_and(wraps_next, c % 2 == 1) if relays else False

        @pl.when(jnp.logical_and(has_next, jnp.logical_not(detour)))
        def _():
            kv_copy(c, 0).start()
            kv_copy(c, 1).start()

        if relays:
            @pl.when(detour)
            def _():
                kv_detour(c, 0).start()
                kv_detour(c, 1).start()

    def turn(kind, g):
        here = pl.ds(pl.multiple_of(g * TILE, TILE), TILE)
        x[kind, here] = jnp.swapaxes(raw[kind, :, here, :], 0, 1)

    for kind in range(4):
        load(kind).wait()

    @pl.loop(0, heads // TILE)
    def _(g):
        turn(0, g)
        turn(1, g)

        @pl.loop(0, group)
        def _(at):
            send_kv(g * group + at)

        turn(2, g)
        turn(3, g)

        @pl.loop(0, group)
        def _(at):
            own_copy(g * group + at).start()
            own_keep(g * group + at).start()

    @pl.when(jnp.logical_not(has_prev))
    def _():
        @pl.loop(0, mine)
        def _(j):
            prev[0, j] = jnp.zeros((2 * rows, width), BF16)
            prev[1, j] = jnp.zeros((2 * rows, width), BF16)

    @pl.when(jnp.logical_not(has_next))
    def _():
        @pl.loop(0, mine)
        def _(j):
            arrived[0, j] = jnp.zeros((2 * rows, width), BF16)
            arrived[1, j] = jnp.zeros((2 * rows, width), BF16)

    row_at = lax.broadcasted_iota(jnp.int32, (2 * rows, 2 * rows), 0)
    column_at = lax.broadcasted_iota(jnp.int32, (2 * rows, 2 * rows), 1)
    sees_own = column_at <= row_at
    sees_prev = column_at > row_at + jnp.where(has_prev, 0, 2 * rows)

    def one_head(j):
        key_prev, value_prev = prev[0, j], prev[1, j]
        key, value, query, grad = own[0, j], own[1, j], own[2, j], own[3, j]
        score_prev = jnp.where(sees_prev, dot_nt(query, key_prev), LOW)
        score_own = jnp.where(sees_own, dot_nt(query, key), LOW)
        top = jnp.maximum(
            jnp.max(score_prev, axis=-1, keepdims=True), jnp.max(score_own, axis=-1, keepdims=True)
        )
        prob_prev = jnp.exp2((score_prev - top) * log2_scale)
        prob_own = jnp.exp2((score_own - top) * log2_scale)
        total = jnp.sum(prob_prev, axis=-1, keepdims=True) + jnp.sum(
            prob_own, axis=-1, keepdims=True
        )
        inverse = 1.0 / total
        prob_prev = prob_prev * inverse
        prob_own = prob_own * inverse
        prob_prev_b = prob_prev.astype(BF16)
        prob_own_b = prob_own.astype(BF16)
        dprob_prev = dot_nt(grad, value_prev)
        dprob_own = dot_nt(grad, value)
        delta = jnp.sum(prob_prev_b.astype(F32) * dprob_prev, axis=-1, keepdims=True) + jnp.sum(
            prob_own_b.astype(F32) * dprob_own, axis=-1, keepdims=True
        )
        dscore_prev = (prob_prev * (dprob_prev - delta)).astype(BF16)
        dscore_own = (prob_own * (dprob_own - delta)).astype(BF16)
        partial[0, j] = (dot_tn(dscore_prev, query) * scale).astype(BF16)
        partial[1, j] = dot_tn(prob_prev_b, grad).astype(BF16)
        staged[0, j] = (
            (dot_nn(dscore_prev, key_prev) + dot_nn(dscore_own, key)) * scale
        ).astype(BF16)
        acc[0, j] = dot_tn(dscore_own, query) * scale
        acc[1, j] = dot_tn(prob_own_b, grad)

    def finish(c):
        @pl.when(has_next)
        def _():
            grad_copy(c, after).wait_recv()

        for at in range(CHUNK):
            j = c * CHUNK + at
            staged[1, j] = (acc[0, j] + arrived[0, j].astype(F32)).astype(BF16)
            staged[2, j] = (acc[1, j] + arrived[1, j].astype(F32)).astype(BF16)
        remote, _, keep = result_out(c)
        remote.start()
        keep.start()

    def forward_grad(c):
        @pl.when(jnp.logical_and(grad_relay, c % 2 == 0))
        def _():
            grad_detour(c).wait_recv()
            grad_forward(c).start()

    @pl.loop(0, chunks)
    def _(c):
        own_arrival(c).wait_recv()
        own_keep(c).wait()

        @pl.when(has_prev)
        def _():
            kv_arrival(c, 0).wait_recv()
            kv_arrival(c, 1).wait_recv()

        for at in range(CHUNK):
            one_head(c * CHUNK + at)

        detour = jnp.logical_and(wraps_prev, c % 2 == 0) if relays else False

        @pl.when(jnp.logical_and(has_prev, jnp.logical_not(detour)))
        def _():
            grad_copy(c, before).start()

        if relays:
            @pl.when(detour)
            def _():
                grad_detour(c).start()

            @pl.when(jnp.logical_and(kv_relay, c % 2 == 0))
            def _():
                for side in range(2):
                    kv_detour(c + 1, side).wait_recv()
                    kv_forward(c + 1, side).start()

        remote, _, keep = query_out(c)
        remote.start()
        keep.start()

        if relays:
            @pl.when(c >= GRAD_LAG)
            def _():
                forward_grad(c - GRAD_LAG)

    if relays:
        @pl.loop(chunks - GRAD_LAG, chunks)
        def _(c):
            forward_grad(c)

    outputs = (grad_query, grad_key, grad_value)

    def turned(kind, g):
        here = pl.ds(pl.multiple_of(g * TILE, TILE), TILE)
        return pltpu.make_async_copy(
            raw.at[kind, :, here], outputs[kind].at[:, here], turned_sem.at[kind, g]
        )

    def turn_back(kind, g):
        here = pl.ds(pl.multiple_of(g * TILE, TILE), TILE)
        raw[kind, :, here] = jnp.swapaxes(out[kind, here], 0, 1)
        turned(kind, g).start()

    def landed(copies):
        _, arrival, keep = copies
        arrival.wait_recv()
        keep.wait()

    def results_back(g):
        @pl.loop(0, group)
        def _(at):
            landed(result_out(g * group + at))

        turn_back(1, g)
        turn_back(2, g)

    groups = heads // TILE

    @pl.loop(0, groups)
    def _(g):
        @pl.loop(0, group)
        def _(at):
            landed(query_out(g * group + at))

        turn_back(0, g)

    @pl.loop(0, groups)
    def _(g):
        @pl.loop(0, group)
        def _(at):
            finish(g * group + at)

        @pl.when(g > 0)
        def _():
            results_back(g - 1)

    results_back(groups - 1)

    @pl.loop(0, groups)
    def _(g):
        for kind in range(3):
            turned(kind, g).wait()

    @pl.loop(0, chunks)
    def _(c):
        own_copy(c).wait_send()

        @pl.when(has_next)
        def _():
            kv_copy(c, 0).wait_send()
            kv_copy(c, 1).wait_send()

        @pl.when(has_prev)
        def _():
            grad_copy(c, before).wait_send()

        if relays:
            @pl.when(jnp.logical_and(kv_relay, c % 2 == 1))
            def _():
                kv_forward(c, 0).wait_send()
                kv_forward(c, 1).wait_send()

            @pl.when(jnp.logical_and(grad_relay, c % 2 == 0))
            def _():
                grad_forward(c).wait_send()

        for copies in (query_out(c), result_out(c)):
            copies[0].wait_send()


def on_device(ctx, inner, query_rows, key_rows, value_rows, grad_rows):
    rows, heads, width = query_rows.shape
    mine = heads // 2
    chunks = mine // CHUNK
    dma = pltpu.SemaphoreType.DMA
    result = pl.pallas_call(
        functools.partial(kernel, (ctx, inner)),
        out_shape=[jax.ShapeDtypeStruct((rows, heads, width), BF16)] * 3,
        in_specs=[pl.BlockSpec(memory_space=pl.ANY)] * 4,
        out_specs=[pl.BlockSpec(memory_space=pl.ANY)] * 3,
        scratch_shapes=[
            pltpu.VMEM((4, rows, heads, width), BF16),
            pltpu.VMEM((4, heads, rows, width), BF16),
            pltpu.VMEM((3, heads, rows, width), BF16),
            pltpu.VMEM((4, mine, 2 * rows, width), BF16),
            pltpu.VMEM((2, mine, 2 * rows, width), BF16),
            pltpu.VMEM((2, mine, 2 * rows, width), F32),
            pltpu.VMEM((2, mine, 2 * rows, width), BF16),
            pltpu.VMEM((2, mine, 2 * rows, width), BF16),
            pltpu.VMEM((3, mine, 2 * rows, width), BF16),
            pltpu.VMEM((2, 2, mine // 2, rows, width), BF16),
            pltpu.VMEM((2, mine // 2, 2 * rows, width), BF16),
            dma((2, chunks)), dma((2, chunks)),
            dma((chunks,)), dma((chunks,)), dma((chunks,)),
            dma((chunks,)), dma((chunks,)),
            dma((chunks,)), dma((chunks,)), dma((chunks,)),
            dma((chunks,)), dma((chunks,)), dma((chunks,)),
            dma((3, chunks // 2)), dma((3, chunks // 2)), dma((4,)), dma((3, heads // TILE)),
        ],
        compiler_params=pltpu.CompilerParams(
            collective_id=0, has_side_effects=True, vmem_limit_bytes=56 * 1024 * 1024
        ),
        cost_estimate=pl.CostEstimate(
            flops=20 * mine * 4 * rows * rows * width,
            bytes_accessed=14 * heads * rows * width,
            transcendentals=mine * 8 * rows * rows,
        ),
    )(key_rows, value_rows, query_rows, grad_rows)
    return tuple(result)


def solution(mesh):
    assert mesh.shape["head"] == 4
    spec = P(("head", "ctx", "inner"), None, None)
    return jax.shard_map(
        functools.partial(on_device, mesh.shape["ctx"], mesh.shape["inner"]),
        mesh=mesh,
        in_specs=(spec,) * 4,
        out_specs=(spec,) * 3,
        check_vma=False,
    )
```

```python
import functools

import jax
import jax.numpy as jnp
from jax import lax
from jax.experimental import pallas as pl
from jax.experimental.pallas import tpu as pltpu
from jax.sharding import PartitionSpec as P

MESH = pl.DeviceIdType.MESH
BF16 = jnp.bfloat16
F32 = jnp.float32
CHUNK = 2
GRAD_LAG = 4
TILE = 16
PARTS = 4
LOW = -1e30


def dot_nt(a, b):
    return lax.dot_general(a, b, (((1,), (1,)), ((), ())), preferred_element_type=F32)


def dot_nn(a, b):
    return lax.dot_general(a, b, (((1,), (0,)), ((), ())), preferred_element_type=F32)


def dot_tn(a, b):
    return lax.dot_general(a, b, (((0,), (0,)), ((), ())), preferred_element_type=F32)


def kernel(
    sizes, key_rows, value_rows, query_rows, grad_rows, grad_query, grad_key, grad_value,
    raw, x, out, own, prev, acc, partial, arrived, staged, relay_kv, relay_grad,
    kv_send, kv_recv, own_send, own_recv, own_local, grad_send, grad_recv,
    query_send, query_recv, query_local, result_send, result_recv, result_local,
    relay_send, relay_recv, raw_sem, turned_sem,
):
    ctx, inner = sizes
    shards = ctx * inner
    heads, rows, width = x.shape[1:]
    mine = heads // 2
    chunks = mine // CHUNK
    group = TILE // 2 // CHUNK
    scale = width ** -0.5
    log2_scale = scale * 1.4426950408889634

    head_at = lax.axis_index("head")
    ctx_at = lax.axis_index("ctx")
    inner_at = lax.axis_index("inner")
    shard = ctx_at * inner + inner_at
    half = head_at % 2
    other = 1 - half
    block = jnp.where(head_at < 2, shard, 2 * shards - 1 - shard)
    has_prev = block > 0
    has_next = block < 2 * shards - 1

    inputs = (key_rows, value_rows, query_rows, grad_rows)

    def load(kind):
        return pltpu.make_async_copy(inputs[kind], raw.at[kind], raw_sem.at[kind])

    def heads_of(side, c):
        return pl.ds((c // group) * TILE + side * (TILE // 2) + (c % group) * CHUNK, CHUNK)

    def device(at, side):
        low = at < shards
        to = jnp.where(low, at, 2 * shards - 1 - at)
        return (jnp.where(low, side, 2 + side), to // inner, to % inner)

    peer = device(block, other)
    after = jnp.where(has_next, block + 1, block - 1)
    before = jnp.where(has_prev, block - 1, block + 1)
    relays = ctx > 1 and inner > 2
    is_first = inner_at == 0
    is_last = inner_at == inner - 1
    low_head = head_at < 2
    can_rise = ctx_at < ctx - 1
    can_fall = ctx_at > 0
    low_corner = jnp.logical_and(is_first, can_rise)
    high_corner = jnp.logical_and(is_last, can_fall)
    wraps_next = jnp.logical_and(has_next, jnp.where(low_head, jnp.logical_and(is_last, can_rise), jnp.logical_and(is_first, can_fall)))
    wraps_prev = jnp.logical_and(has_prev, jnp.where(low_head, jnp.logical_and(is_first, can_fall), jnp.logical_and(is_last, can_rise)))
    kv_relay = jnp.where(low_head, high_corner, low_corner)
    grad_relay = jnp.where(low_head, low_corner, high_corner)
    mirror = inner - 1 - inner_at
    my_rows = pl.ds(pl.multiple_of(half * rows, rows), rows)
    peer_rows = pl.ds(pl.multiple_of(other * rows, rows), rows)

    def kv_copy(c, side):
        return pltpu.make_async_remote_copy(
            x.at[pl.ds(0, 2), heads_of(side, c)],
            prev.at[:, pl.ds(c * CHUNK, CHUNK), my_rows],
            kv_send.at[side, c], kv_recv.at[half, c], device(after, side), MESH,
        )

    def relay_at(c):
        return pl.ds((c // 2) * CHUNK, CHUNK)

    def kv_detour(c, side):
        return pltpu.make_async_remote_copy(
            x.at[pl.ds(0, 2), heads_of(side, c)],
            relay_kv.at[side, :, relay_at(c)],
            kv_send.at[side, c], relay_recv.at[side, c // 2],
            (head_at, jnp.where(low_head, ctx_at + 1, ctx_at - 1), inner_at), MESH,
        )

    def kv_forward(c, side):
        return pltpu.make_async_remote_copy(
            relay_kv.at[side, :, relay_at(c)],
            prev.at[:, pl.ds(c * CHUNK, CHUNK), my_rows],
            relay_send.at[side, c // 2], kv_recv.at[half, c],
            (head_at - half + side, ctx_at, mirror), MESH,
        )

    def grad_detour(c):
        return pltpu.make_async_remote_copy(
            partial.at[:, pl.ds(c * CHUNK, CHUNK)],
            relay_grad.at[:, relay_at(c)],
            grad_send.at[c], relay_recv.at[2, c // 2],
            (head_at, jnp.where(low_head, ctx_at - 1, ctx_at + 1), inner_at), MESH,
        )

    def grad_forward(c):
        return pltpu.make_async_remote_copy(
            relay_grad.at[:, relay_at(c)],
            arrived.at[:, pl.ds(c * CHUNK, CHUNK)],
            relay_send.at[2, c // 2], grad_recv.at[c],
            (head_at, ctx_at, mirror), MESH,
        )

    def kv_arrival(c, side):
        return pltpu.make_async_remote_copy(
            x.at[pl.ds(0, 2), heads_of(side, c)],
            prev.at[:, pl.ds(c * CHUNK, CHUNK), pl.ds(side * rows, rows)],
            kv_send.at[side, c], kv_recv.at[side, c], device(before, side), MESH,
        )

    def own_copy(c):
        return pltpu.make_async_remote_copy(
            x.at[:, heads_of(other, c)],
            own.at[:, pl.ds(c * CHUNK, CHUNK), my_rows],
            own_send.at[c], own_recv.at[c], peer, MESH,
        )

    def own_arrival(c):
        return pltpu.make_async_remote_copy(
            x.at[:, heads_of(other, c)],
            own.at[:, pl.ds(c * CHUNK, CHUNK), peer_rows],
            own_send.at[c], own_recv.at[c], peer, MESH,
        )

    def own_keep(c):
        return pltpu.make_async_copy(
            x.at[:, heads_of(half, c)],
            own.at[:, pl.ds(c * CHUNK, CHUNK), my_rows],
            own_local.at[c],
        )

    def grad_copy(c, to):
        return pltpu.make_async_remote_copy(
            partial.at[:, pl.ds(c * CHUNK, CHUNK)],
            arrived.at[:, pl.ds(c * CHUNK, CHUNK)],
            grad_send.at[c], grad_recv.at[c], device(to, half), MESH,
        )

    def out_copies(c, first, count, send, recv, local):
        kinds = pl.ds(first, count)
        here = pl.ds(c * CHUNK, CHUNK)
        remote = pltpu.make_async_remote_copy(
            staged.at[kinds, here, peer_rows],
            out.at[kinds, heads_of(half, c)],
            send.at[c], recv.at[c], peer, MESH,
        )
        arrival = pltpu.make_async_remote_copy(
            staged.at[kinds, here, peer_rows],
            out.at[kinds, heads_of(other, c)],
            send.at[c], recv.at[c], peer, MESH,
        )
        keep = pltpu.make_async_copy(
            staged.at[kinds, here, my_rows],
            out.at[kinds, heads_of(half, c)],
            local.at[c],
        )
        return remote, arrival, keep

    def query_out(c):
        return out_copies(c, 0, 1, query_send, query_recv, query_local)

    def result_out(c):
        return out_copies(c, 1, 2, result_send, result_recv, result_local)

    for kind in range(4):
        load(kind).start()

    barrier = pltpu.get_barrier_semaphore()
    pl.semaphore_signal(barrier, inc=1, device_id=peer, device_id_type=MESH)

    @pl.when(has_next)
    def _():
        for side in range(2):
            pl.semaphore_signal(barrier, inc=1, device_id=device(after, side), device_id_type=MESH)

    @pl.when(has_prev)
    def _():
        for side in range(2):
            pl.semaphore_signal(barrier, inc=1, device_id=device(before, side), device_id_type=MESH)

    greeted = 1 + jnp.where(has_next, 2, 0) + jnp.where(has_prev, 2, 0)
    if relays:
        corner = jnp.logical_or(is_first, is_last)
        rises = jnp.logical_and(corner, can_rise)
        falls = jnp.logical_and(corner, can_fall)

        @pl.when(corner)
        def _():
            for side in range(2):
                pl.semaphore_signal(
                    barrier, inc=1, device_id=(head_at - half + side, ctx_at, mirror),
                    device_id_type=MESH,
                )

        @pl.when(rises)
        def _():
            pl.semaphore_signal(
                barrier, inc=1, device_id=(head_at, ctx_at + 1, inner_at), device_id_type=MESH
            )

        @pl.when(falls)
        def _():
            pl.semaphore_signal(
                barrier, inc=1, device_id=(head_at, ctx_at - 1, inner_at), device_id_type=MESH
            )

        greeted = greeted + jnp.where(corner, 2, 0)
        greeted = greeted + jnp.where(rises, 1, 0) + jnp.where(falls, 1, 0)
    pl.semaphore_wait(barrier, greeted)

    def send_kv(c):
        detour = jnp.logical_and(wraps_next, c % 2 == 1) if relays else False

        @pl.when(jnp.logical_and(has_next, jnp.logical_not(detour)))
        def _():
            kv_copy(c, 0).start()
            kv_copy(c, 1).start()

        if relays:
            @pl.when(detour)
            def _():
                kv_detour(c, 0).start()
                kv_detour(c, 1).start()

    def turn(kind, g):
        here = pl.ds(pl.multiple_of(g * TILE, TILE), TILE)
        x[kind, here] = jnp.swapaxes(raw[kind, :, here, :], 0, 1)

    for kind in range(4):
        load(kind).wait()

    @pl.loop(0, heads // TILE)
    def _(g):
        turn(0, g)
        turn(1, g)

        @pl.loop(0, group)
        def _(at):
            send_kv(g * group + at)

        turn(2, g)
        turn(3, g)

        @pl.loop(0, group)
        def _(at):
            own_copy(g * group + at).start()
            own_keep(g * group + at).start()

    @pl.when(jnp.logical_not(has_prev))
    def _():
        @pl.loop(0, mine)
        def _(j):
            prev[0, j] = jnp.zeros((2 * rows, width), BF16)
            prev[1, j] = jnp.zeros((2 * rows, width), BF16)

    @pl.when(jnp.logical_not(has_next))
    def _():
        @pl.loop(0, mine)
        def _(j):
            arrived[0, j] = jnp.zeros((2 * rows, width), BF16)
            arrived[1, j] = jnp.zeros((2 * rows, width), BF16)

    row_at = lax.broadcasted_iota(jnp.int32, (2 * rows, 2 * rows), 0)
    column_at = lax.broadcasted_iota(jnp.int32, (2 * rows, 2 * rows), 1)
    sees_own = column_at <= row_at
    sees_prev = column_at > row_at + jnp.where(has_prev, 0, 2 * rows)

    def one_head(j):
        key_prev, value_prev = prev[0, j], prev[1, j]
        key, value, query, grad = own[0, j], own[1, j], own[2, j], own[3, j]
        score_prev = jnp.where(sees_prev, dot_nt(query, key_prev), LOW)
        score_own = jnp.where(sees_own, dot_nt(query, key), LOW)
        top = jnp.maximum(
            jnp.max(score_prev, axis=-1, keepdims=True), jnp.max(score_own, axis=-1, keepdims=True)
        )
        prob_prev = jnp.exp2((score_prev - top) * log2_scale)
        prob_own = jnp.exp2((score_own - top) * log2_scale)
        total = jnp.sum(prob_prev, axis=-1, keepdims=True) + jnp.sum(
            prob_own, axis=-1, keepdims=True
        )
        inverse = 1.0 / total
        prob_prev = prob_prev * inverse
        prob_own = prob_own * inverse
        prob_prev_b = prob_prev.astype(BF16)
        prob_own_b = prob_own.astype(BF16)
        dprob_prev = dot_nt(grad, value_prev)
        dprob_own = dot_nt(grad, value)
        delta = jnp.sum(prob_prev_b.astype(F32) * dprob_prev, axis=-1, keepdims=True) + jnp.sum(
            prob_own_b.astype(F32) * dprob_own, axis=-1, keepdims=True
        )
        dscore_prev = (prob_prev * (dprob_prev - delta)).astype(BF16)
        dscore_own = (prob_own * (dprob_own - delta)).astype(BF16)
        partial[0, j] = (dot_tn(dscore_prev, query) * scale).astype(BF16)
        partial[1, j] = dot_tn(prob_prev_b, grad).astype(BF16)
        staged[0, j] = (
            (dot_nn(dscore_prev, key_prev) + dot_nn(dscore_own, key)) * scale
        ).astype(BF16)
        acc[0, j] = dot_tn(dscore_own, query) * scale
        acc[1, j] = dot_tn(prob_own_b, grad)

    def finish(c):
        @pl.when(has_next)
        def _():
            grad_copy(c, after).wait_recv()

        for at in range(CHUNK):
            j = c * CHUNK + at
            staged[1, j] = (acc[0, j] + arrived[0, j].astype(F32)).astype(BF16)
            staged[2, j] = (acc[1, j] + arrived[1, j].astype(F32)).astype(BF16)
        remote, _, keep = result_out(c)
        remote.start()
        keep.start()

    def forward_grad(c):
        @pl.when(jnp.logical_and(grad_relay, c % 2 == 0))
        def _():
            grad_detour(c).wait_recv()
            grad_forward(c).start()

    @pl.loop(0, chunks)
    def _(c):
        own_arrival(c).wait_recv()
        own_keep(c).wait()

        @pl.when(has_prev)
        def _():
            kv_arrival(c, 0).wait_recv()
            kv_arrival(c, 1).wait_recv()

        for at in range(CHUNK):
            one_head(c * CHUNK + at)

        detour = jnp.logical_and(wraps_prev, c % 2 == 0) if relays else False

        @pl.when(jnp.logical_and(has_prev, jnp.logical_not(detour)))
        def _():
            grad_copy(c, before).start()

        if relays:
            @pl.when(detour)
            def _():
                grad_detour(c).start()

            @pl.when(jnp.logical_and(kv_relay, c % 2 == 0))
            def _():
                for side in range(2):
                    kv_detour(c + 1, side).wait_recv()
                    kv_forward(c + 1, side).start()

        remote, _, keep = query_out(c)
        remote.start()
        keep.start()

        if relays:
            @pl.when(c >= GRAD_LAG)
            def _():
                forward_grad(c - GRAD_LAG)

    if relays:
        @pl.loop(chunks - GRAD_LAG, chunks)
        def _(c):
            forward_grad(c)

    outputs = (grad_query, grad_key, grad_value)

    def turned(kind, g):
        here = pl.ds(pl.multiple_of(g * TILE, TILE), TILE)
        return pltpu.make_async_copy(
            raw.at[kind, :, here], outputs[kind].at[:, here], turned_sem.at[kind, g]
        )

    def turn_back(kind, g):
        here = pl.ds(pl.multiple_of(g * TILE, TILE), TILE)
        raw[kind, :, here] = jnp.swapaxes(out[kind, here], 0, 1)
        turned(kind, g).start()

    def landed(copies):
        _, arrival, keep = copies
        arrival.wait_recv()
        keep.wait()

    def results_back(g):
        @pl.loop(0, group)
        def _(at):
            landed(result_out(g * group + at))

        turn_back(1, g)
        turn_back(2, g)

    groups = heads // TILE

    @pl.loop(0, groups)
    def _(g):
        @pl.loop(0, group)
        def _(at):
            landed(query_out(g * group + at))

        turn_back(0, g)

    @pl.loop(0, groups)
    def _(g):
        @pl.loop(0, group)
        def _(at):
            finish(g * group + at)

        @pl.when(g > 0)
        def _():
            results_back(g - 1)

    results_back(groups - 1)

    @pl.loop(0, groups)
    def _(g):
        for kind in range(3):
            turned(kind, g).wait()

    @pl.loop(0, chunks)
    def _(c):
        own_copy(c).wait_send()

        @pl.when(has_next)
        def _():
            kv_copy(c, 0).wait_send()
            kv_copy(c, 1).wait_send()

        @pl.when(has_prev)
        def _():
            grad_copy(c, before).wait_send()

        if relays:
            @pl.when(jnp.logical_and(kv_relay, c % 2 == 1))
            def _():
                kv_forward(c, 0).wait_send()
                kv_forward(c, 1).wait_send()

            @pl.when(jnp.logical_and(grad_relay, c % 2 == 0))
            def _():
                grad_forward(c).wait_send()

        for copies in (query_out(c), result_out(c)):
            copies[0].wait_send()


def hand_over(*refs):
    kinds = len(refs) // 2
    sem = refs[-1]
    copies = []
    for kind in range(kinds):
        source, target = refs[kind], refs[kinds + kind]
        count = source.shape[0] // PARTS
        for part in range(PARTS):
            here = pl.ds(part * count, count)
            copies.append(
                pltpu.make_async_copy(source.at[here], target.at[here], sem.at[kind, part])
            )
    for copy in copies:
        copy.start()
    for copy in copies:
        copy.wait()


def on_device(ctx, inner, query_rows, key_rows, value_rows, grad_rows):
    rows, heads, width = query_rows.shape
    mine = heads // 2
    chunks = mine // CHUNK
    dma = pltpu.SemaphoreType.DMA
    result = pl.pallas_call(
        functools.partial(kernel, (ctx, inner)),
        out_shape=[jax.ShapeDtypeStruct((rows, heads, width), BF16)] * 3,
        in_specs=[pl.BlockSpec(memory_space=pl.ANY)] * 4,
        out_specs=[pl.BlockSpec(memory_space=pl.ANY)] * 3,
        scratch_shapes=[
            pltpu.VMEM((4, rows, heads, width), BF16),
            pltpu.VMEM((4, heads, rows, width), BF16),
            pltpu.VMEM((3, heads, rows, width), BF16),
            pltpu.VMEM((4, mine, 2 * rows, width), BF16),
            pltpu.VMEM((2, mine, 2 * rows, width), BF16),
            pltpu.VMEM((2, mine, 2 * rows, width), F32),
            pltpu.VMEM((2, mine, 2 * rows, width), BF16),
            pltpu.VMEM((2, mine, 2 * rows, width), BF16),
            pltpu.VMEM((3, mine, 2 * rows, width), BF16),
            pltpu.VMEM((2, 2, mine // 2, rows, width), BF16),
            pltpu.VMEM((2, mine // 2, 2 * rows, width), BF16),
            dma((2, chunks)), dma((2, chunks)),
            dma((chunks,)), dma((chunks,)), dma((chunks,)),
            dma((chunks,)), dma((chunks,)),
            dma((chunks,)), dma((chunks,)), dma((chunks,)),
            dma((chunks,)), dma((chunks,)), dma((chunks,)),
            dma((3, chunks // 2)), dma((3, chunks // 2)), dma((4,)), dma((3, heads // TILE)),
        ],
        compiler_params=pltpu.CompilerParams(
            collective_id=0, has_side_effects=True, vmem_limit_bytes=56 * 1024 * 1024
        ),
        cost_estimate=pl.CostEstimate(
            flops=20 * mine * 4 * rows * rows * width,
            bytes_accessed=14 * heads * rows * width,
            transcendentals=mine * 8 * rows * rows,
        ),
    )(key_rows, value_rows, query_rows, grad_rows)
    kinds = len(result)
    return tuple(
        pl.pallas_call(
            hand_over,
            out_shape=[jax.ShapeDtypeStruct((rows, heads, width), BF16)] * kinds,
            in_specs=[pl.BlockSpec(memory_space=pl.ANY)] * kinds,
            out_specs=[pl.BlockSpec(memory_space=pl.ANY)] * kinds,
            scratch_shapes=[dma((kinds, PARTS))],
        )(*result)
    )


def solution(mesh):
    assert mesh.shape["head"] == 4
    spec = P(("head", "ctx", "inner"), None, None)
    return jax.shard_map(
        functools.partial(on_device, mesh.shape["ctx"], mesh.shape["inner"]),
        mesh=mesh,
        in_specs=(spec,) * 4,
        out_specs=(spec,) * 3,
        check_vma=False,
    )
```
